32 devices in a mesh: win: 2 (over x), wide: 8 (over z, y), narrow: 2 (over core).
Axes of the slice: x: 2, y: 2, z: 4, core: 2. Of those that a mesh axis runs over, the one named last changes fastest.
Arguments:
- window_data: float32 [384, 128, 256], P(('win', 'wide'), 'narrow'), parts along dimension 0, may hold values from -6 to 6
- factor_one: float32 [256, 48], P(('win', 'narrow')), parts along dimension 0, may hold values from -0.5 to 0.5
- factor_two: float32 [512, 48], P('win'), parts along dimension 0, may hold values from -0.375 to 0.375
- factor_three: float32 [384, 48], P(('win', 'wide')), parts along dimension 0, may hold values from -0.4375 to 0.4375
Outputs:
- basis_one: float32 [256, 48], P(('win', 'narrow')), parts along dimension 0
- basis_two: float32 [512, 48], P('win'), parts along dimension 0
- basis_three: float32 [384, 48], P(('win', 'wide')), parts along dimension 0
- core_unfolded: float32 [48, 4608], P(None, ('win', 'wide', 'narrow')), parts along dimension 1
The draws below stay inside these ranges and needn't reach their ends.
There are 2 independent parts, one for each index of `win`. The reference program is written for one: setup_inputs(seed, part) draws one part's arguments, and reference() takes and returns one part's arrays. A program takes and returns all parts, laid end to end along the dimension named above; each array names one. Nothing has to cross between parts.
All inputs are finite; a program needn't handle non-finite values.
Results may differ from the reference program's by a relative error of at most 0.0003.
Values sent between devices are 32-bit elements; how exact they have to be, the bound alone decides.
A program may use at most 64 MiB of HBM per device.

```python
import jax
import jax.numpy as jnp
from jax import lax

R = 48
I2 = 256
I1 = 128
I3 = 192


def levels(key, dims, pieces, low, high):
    gain = 1.0
    for axis_at, blocks in pieces:
        steps = jax.random.uniform(jax.random.fold_in(jax.random.fold_in(key, 6), axis_at), (blocks,), jnp.float32, low / len(pieces), high / len(pieces))
        gain = gain * jnp.repeat(jnp.exp(steps), dims[axis_at] // blocks).reshape((-1,) + (1,) * (len(dims) - 1 - axis_at))
    return gain


def normal_values(key, shape, scale, reach, cuts=(), kind=jnp.bfloat16):
    entries = scale * jax.random.normal(key, shape, jnp.float32)
    if cuts:
        entries = entries * levels(key, shape, cuts, -0.22, 0.18)
    return jnp.clip(entries, -reach, reach).astype(kind)


def setup_inputs(seed: int = 0, part: int = 0) -> dict:
    seeds = jax.random.split(jax.random.key(seed), 5)
    part_splits = jax.random.split(jax.random.fold_in(seeds[4], part), 5)
    window_data = normal_values(part_splits[0], (I3, I1, I2), 1.0, 6.0, ((0, 8), (1, 2)), jnp.float32)
    factor_one = normal_values(part_splits[1], (I1, R), I1 ** -0.5, 0.5, ((0, 2),), jnp.float32)
    factor_two = normal_values(part_splits[2], (I2, R), I2 ** -0.5, 0.375, (), jnp.float32)
    factor_three = normal_values(part_splits[3], (I3, R), I3 ** -0.5, 0.4375, ((0, 8),), jnp.float32)
    return {"window_data": window_data, "factor_one": factor_one, "factor_two": factor_two, "factor_three": factor_three}


highest = lax.Precision.HIGHEST

def contract(form, left, right):
    return jnp.einsum(form, left, right, precision=highest)

def orthonormal(basis):
    gram = jnp.dot(basis.T, basis, precision=highest)
    lower = jnp.linalg.cholesky(gram)
    return lax.linalg.triangular_solve(lower, basis, left_side=False, lower=True, transpose_a=True)

def reference(window_data, factor_one, factor_two, factor_three):
    along_two = contract('kij,jb->kib', window_data, factor_two)
    unfold_one = contract('kib,kc->ibc', along_two, factor_three)
    weights_one = contract('ibc,ia->bca', unfold_one, factor_one)
    basis_one = orthonormal(contract('ibc,bca->ia', unfold_one, weights_one))
    along_one = contract('kij,ia->kaj', window_data, basis_one)
    unfold_two = contract('kaj,kc->jac', along_one, factor_three)
    weights_two = contract('jac,jb->acb', unfold_two, factor_two)
    basis_two = orthonormal(contract('jac,acb->jb', unfold_two, weights_two))
    along_new = contract('kij,jb->kib', window_data, basis_two)
    unfold_three = contract('kib,ia->kab', along_new, basis_one)
    weights_three = contract('kab,kc->abc', unfold_three, factor_three)
    basis_three = orthonormal(contract('kab,abc->kc', unfold_three, weights_three))
    core = contract('kab,kc->abc', unfold_three, basis_three).reshape(R, R * R)
    return (basis_one, basis_two, basis_three, core)
```

```python
import functools

import jax
import jax.numpy as jnp
from jax import lax
from jax.experimental import pallas as pl
from jax.experimental.pallas import tpu as pltpu
from jax.sharding import PartitionSpec as P

highest = lax.Precision.HIGHEST
vmem = pl.BlockSpec(memory_space=pltpu.VMEM)


def contract(form, left, right):
    return jnp.einsum(form, left, right, precision=highest)


def dot(left, right):
    return jnp.dot(left, right, precision=highest, preferred_element_type=jnp.float32)


def dot_t(left, right):
    return lax.dot_general(
        left, right, (((0,), (0,)), ((), ())), precision=highest, preferred_element_type=jnp.float32
    )


def dot_rt(left, right):
    return lax.dot_general(
        left, right, (((1,), (1,)), ((), ())), precision=highest, preferred_element_type=jnp.float32
    )


def inverse_lower(gram):
    rank = gram.shape[0]
    group = 8
    rows = lax.broadcasted_iota(jnp.int32, (rank, rank), 0)
    columns = lax.broadcasted_iota(jnp.int32, (rank, rank), 1)
    both = jnp.concatenate([gram, (rows == columns).astype(jnp.float32)], axis=1)
    blocks = [both[at : at + group] for at in range(0, rank, group)]
    inside = lax.broadcasted_iota(jnp.int32, (group, 2 * rank), 0)
    scales = []
    for step in range(rank):
        at, row = divmod(step, group)
        pivot_row = blocks[at][row : row + 1]
        pivot = pivot_row[:, step : step + 1]
        scales.append(lax.rsqrt(pivot))
        scaled = pivot_row * (1.0 / pivot)
        for later in range(at, rank // group):
            change = blocks[later][:, step : step + 1] * scaled
            if later == at:
                change = jnp.where(inside > row, change, 0.0)
            blocks[later] = blocks[later] - change
    right = jnp.concatenate(blocks, axis=0)[:, rank:]
    return right * jnp.concatenate(scales, axis=0)


class Link:
    def __init__(self, wide, narrow, send, recv):
        self.wide, self.narrow = wide, narrow
        self.send, self.recv = send, recv
        self.used = 0
        self.started = []
        self.w = lax.axis_index("wide")
        self.n = lax.axis_index("narrow")

    def others(self):
        for step in range(1, self.wide * self.narrow):
            dw, dn = divmod(step, self.narrow)
            yield lax.rem(self.w + dw, self.wide), lax.rem(self.n + dn, self.narrow)

    def greet(self):
        barrier = pltpu.get_barrier_semaphore()
        for w, n in self.others():
            pl.semaphore_signal(
                barrier, inc=1, device_id={"wide": w, "narrow": n}, device_id_type=pl.DeviceIdType.MESH
            )
        pl.semaphore_wait(barrier, self.wide * self.narrow - 1)

    def put(self, source, target, w, n):
        copy = pltpu.make_async_remote_copy(
            src_ref=source,
            dst_ref=target,
            send_sem=self.send.at[self.used],
            recv_sem=self.recv.at[self.used],
            device_id={"wide": w, "narrow": n},
            device_id_type=pl.DeviceIdType.MESH,
        )
        self.used += 1
        copy.start()
        self.started.append(copy)
        return copy

    def along_wide(self):
        return [(step, lax.rem(self.w + step, self.wide)) for step in range(1, self.wide)]

    def close(self):
        for copy in self.started:
            copy.wait_send()


def mode_one_kernel(wide, narrow, u_ref, f_ref, basis_ref, core_ref,
                    parts, total, w_send, w_recv, p_send, p_recv, p_all, c_part, c_recv, c_all, send, recv):
    link = Link(wide, narrow, send, recv)
    share = total.shape[1]
    rows = f_ref.shape[0]
    rank = f_ref.shape[1]
    per = rank // wide
    chunk = rows // wide
    half = rank // narrow
    link.greet()
    partner = lax.rem(link.n + 1, narrow)
    copies = []
    for step, w in link.along_wide():
        columns = pl.ds(pl.multiple_of(w * share, 128), share)
        copies.append(link.put(u_ref.at[:, columns], parts.at[step - 1], w, link.n))
    added = u_ref[:, pl.ds(pl.multiple_of(link.w * share, 128), share)]
    for step, copy in enumerate(copies):
        copy.wait_recv()
        added = added + parts[step]
    total[...] = added
    factor = f_ref[...]
    for v in range(per):
        w_send[v] = dot(total[:, v * rows : (v + 1) * rows], factor)
    copy = link.put(w_send, w_recv, link.w, partner)
    copy.wait_recv()
    product = jnp.zeros((rows, rank), jnp.float32)
    for v in range(per):
        product = product + dot_t(total[:, v * rows : (v + 1) * rows], w_send[v] + w_recv[v])
    for w in range(wide):
        p_send[w] = product[w * chunk : (w + 1) * chunk]
    copies = [link.put(p_send.at[w], p_recv.at[step - 1], w, link.n) for step, w in link.along_wide()]
    added = p_send[link.w]
    for step, copy in enumerate(copies):
        copy.wait_recv()
        added = added + p_recv[step]
    mine = link.n * wide + link.w
    p_all[mine] = added
    copies = [link.put(p_all.at[mine], p_all.at[mine], w, n) for w, n in link.others()]
    for copy in copies:
        copy.wait_recv()
    whole = p_all[...].reshape(narrow * rows, rank)
    inverse = inverse_lower(dot_t(whole, whole))
    basis = dot_rt(p_all[pl.ds(link.n * wide, wide)].reshape(rows, rank), inverse)
    basis_ref[...] = basis
    for v in range(per):
        c_part[:, v * rank : (v + 1) * rank] = dot(total[:, v * rows : (v + 1) * rows], basis)
    theirs = pl.ds(pl.multiple_of(partner * half, 8), half)
    copy = link.put(c_part.at[theirs, :], c_recv, link.w, partner)
    own = c_part[pl.ds(pl.multiple_of(link.n * half, 8), half), :]
    copy.wait_recv()
    c_all[link.w, link.n] = own + c_recv[...]
    block = c_all.at[link.w, link.n]
    copies = [link.put(block, block, w, link.n) for _, w in link.along_wide()]
    passed = [link.put(block, block, link.w, partner)]
    for (step, _), copy in zip(link.along_wide(), copies):
        copy.wait_recv()
        source = lax.rem(link.w + wide - step, wide)
        block = c_all.at[source, link.n]
        passed.append(link.put(block, block, link.w, partner))
    for copy in passed:
        copy.wait_recv()
    for w in range(wide):
        for n in range(narrow):
            core_ref[w, n * half : (n + 1) * half] = c_all[w, n]
    link.close()


def mode_two_kernel(wide, narrow, p_ref, basis_ref, p_recv, p_all, send, recv):
    link = Link(wide, narrow, send, recv)
    group = wide * narrow
    link.greet()
    copies = [
        link.put(p_ref.at[w * narrow + n], p_recv.at[step], w, n)
        for step, (w, n) in enumerate(link.others())
    ]
    mine = link.w * narrow + link.n
    added = p_ref[mine]
    for step, copy in enumerate(copies):
        copy.wait_recv()
        added = added + p_recv[step]
    p_all[mine] = added
    copies = [link.put(p_all.at[mine], p_all.at[mine], w, n) for w, n in link.others()]
    for copy in copies:
        copy.wait_recv()
    whole = p_all[...].reshape(basis_ref.shape)
    basis_ref[...] = dot_rt(whole, inverse_lower(dot_t(whole, whole)))
    link.close()


def mode_three_kernel(wide, narrow, u_ref, basis_ref, core_ref, u_all, p_send, p_recv, p_all, send, recv):
    link = Link(wide, narrow, send, recv)
    group = wide * narrow
    rows, rank = basis_ref.shape
    share = core_ref.shape[0]
    link.greet()
    copies = [
        link.put(u_ref.at[w * narrow + n], u_all.at[link.n, link.w], w, n) for w, n in link.others()
    ]
    u_all[link.n, link.w] = u_ref[link.w * narrow + link.n]
    for copy in copies:
        copy.wait_recv()
    factor = u_all[0, :, :, share:].reshape(wide * rows, rank)
    unfold = u_all[0, :, :, :share]
    for n in range(1, narrow):
        unfold = unfold + u_all[n, :, :, :share]
    unfold = unfold.reshape(wide * rows, share)
    product = dot(unfold, dot_t(unfold, factor))
    p_send[...] = product.reshape(wide, rows, rank)
    copies = [link.put(p_send.at[w], p_recv.at[step - 1], w, link.n) for step, w in link.along_wide()]
    added = p_send[link.w]
    for step, copy in enumerate(copies):
        copy.wait_recv()
        added = added + p_recv[step]
    p_all[link.n, link.w] = added
    block = p_all.at[link.n, link.w]
    copies = [link.put(block, block, w, n) for w, n in link.others()]
    for copy in copies:
        copy.wait_recv()
    whole = p_all[0]
    for n in range(1, narrow):
        whole = whole + p_all[n]
    p_recv[...] = whole
    whole = whole.reshape(wide * rows, rank)
    inverse = inverse_lower(dot_t(whole, whole))
    basis_ref[...] = dot_rt(p_recv[link.w], inverse)
    core_ref[...] = dot_t(unfold, dot_rt(whole, inverse))
    link.close()


def call(kernel, wide, narrow, outs, scratch, copies, at, operands):
    return pl.pallas_call(
        functools.partial(kernel, wide, narrow),
        out_shape=[jax.ShapeDtypeStruct(shape, jnp.float32) for shape in outs],
        in_specs=[vmem] * len(operands),
        out_specs=[vmem] * len(outs),
        scratch_shapes=[pltpu.VMEM(shape, jnp.float32) for shape in scratch]
        + [pltpu.SemaphoreType.DMA((copies,))] * 2,
        compiler_params=pltpu.CompilerParams(
            collective_id=at, has_side_effects=True, vmem_limit_bytes=32 * 1024 * 1024
        ),
    )(*operands)


def on_device(wide, narrow, window_data, factor_one, factor_two, factor_three):
    layers, rows, cells = window_data.shape
    rank = factor_one.shape[1]
    group = wide * narrow
    per = rank // wide
    share = per * rows
    along_two = contract("kij,jb->kbi", window_data, factor_two).reshape(layers, rank * rows)
    unfold_one = contract("kc,kn->cn", factor_three, along_two)
    basis_one, core_two = call(
        mode_one_kernel, wide, narrow,
        [(rows, rank), (wide, rank, per * rank)],
        [
            (wide - 1, rank, share), (rank, share),
            (per, rank, rank), (per, rank, rank),
            (wide, rows // wide, rank), (wide - 1, rows // wide, rank), (group, rows // wide, rank),
            (rank, per * rank), (rank // narrow, per * rank), (wide, narrow, rank // narrow, per * rank),
        ],
        4 * (wide - 1) + 3 + group - 1, 0, (unfold_one, factor_one),
    )
    core_two = core_two.reshape(wide, rank, per, rank)
    along_one = contract("kij,ia->kaj", window_data, basis_one)
    spread_two = contract("wcva,kc->kawv", core_two, factor_three).reshape(layers, rank, rank)
    product_two = contract("kaj,kab->jb", along_one, spread_two)
    basis_two, = call(
        mode_two_kernel, wide, narrow,
        [(cells, rank)],
        [(group - 1, cells // group, rank), (group, cells // group, rank)],
        2 * (group - 1), 1, (product_two.reshape(group, cells // group, rank),),
    )
    along_new = contract("kij,jb->kib", window_data, basis_two)
    unfold_three = contract("kib,ia->kba", along_new, basis_one)
    shares = rank // group * rank
    unfold_three = unfold_three.reshape(layers, group, shares)
    unfold_three = jnp.concatenate(
        [unfold_three, jnp.broadcast_to(factor_three[:, None], (layers, group, rank))], axis=2
    ).transpose(1, 0, 2)
    basis_three, core = call(
        mode_three_kernel, wide, narrow,
        [(layers, rank), (shares, rank)],
        [
            (narrow, wide, layers, shares + rank),
            (wide, layers, rank), (wide, layers, rank), (narrow, wide, layers, rank),
        ],
        2 * (group - 1) + wide - 1, 2, (unfold_three,),
    )
    core = core.reshape(rank // group, rank, rank).transpose(1, 0, 2).reshape(rank, shares)
    return basis_one, basis_two, basis_three, core


def orthonormal(basis, gram):
    lower = jnp.linalg.cholesky(gram)
    return lax.linalg.triangular_solve(lower, basis, left_side=False, lower=True, transpose_a=True)


def full_core(partial_value):
    flat = partial_value.reshape(
        partial_value.shape[0], partial_value.shape[1] * partial_value.shape[2]
    )
    shares = lax.psum_scatter(flat, ("wide", "narrow"), scatter_dimension=1, tiled=True)
    whole = lax.all_gather(shares, ("wide", "narrow"), axis=1, tiled=True)
    return whole.reshape(partial_value.shape)


def plain_on_device(window_data, factor_one, factor_two, factor_three):
    rank = factor_one.shape[1]
    along_two = contract("kij,jb->kib", window_data, factor_two)
    unfold_part = contract("kib,kc->ibc", along_two, factor_three).reshape(
        along_two.shape[1], rank * rank
    )
    unfold_rows = lax.psum_scatter(unfold_part, "wide", scatter_dimension=1, tiled=True)
    weights_one = lax.psum(jnp.dot(unfold_rows.T, factor_one, precision=highest), "narrow")
    product_one = lax.psum(jnp.dot(unfold_rows, weights_one, precision=highest), "wide")
    gram_one = lax.psum(jnp.dot(product_one.T, product_one, precision=highest), "narrow")
    basis_one = orthonormal(product_one, gram_one)
    along_one = contract("kij,ia->kaj", window_data, basis_one)
    core_two = full_core(
        contract("kab,kc->abc", contract("kaj,jb->kab", along_one, factor_two), factor_three)
    )
    spread_two = contract("abc,kc->kab", core_two, factor_three)
    product_two = lax.psum(contract("kaj,kab->jb", along_one, spread_two), ("wide", "narrow"))
    basis_two = orthonormal(product_two, jnp.dot(product_two.T, product_two, precision=highest))
    along_new = contract("kij,jb->kib", window_data, basis_two)
    unfold_three = contract("kib,ia->kab", along_new, basis_one)
    core_three = full_core(contract("kab,kc->abc", unfold_three, factor_three))
    product_three = lax.psum(contract("kab,abc->kc", unfold_three, core_three), "narrow")
    gram_three = lax.psum(jnp.dot(product_three.T, product_three, precision=highest), "wide")
    basis_three = orthonormal(product_three, gram_three)
    core_part = contract("kab,kc->abc", unfold_three, basis_three).reshape(rank, rank * rank)
    core_shares = lax.psum_scatter(core_part, ("wide", "narrow"), scatter_dimension=1, tiled=True)
    return (basis_one, basis_two, basis_three, core_shares)


def program(wide, narrow, window_data, factor_one, factor_two, factor_three):
    layers, rows, cells = window_data.shape
    rank = factor_one.shape[1]
    group = wide * narrow
    even = (
        narrow == 2
        and rank % (8 * narrow) == 0
        and rank % group == 0
        and (rank // wide * rows) % 128 == 0
        and rows % (8 * wide) == 0
        and cells % (8 * group) == 0
        and layers % 8 == 0
    )
    body = functools.partial(on_device, wide, narrow) if even else plain_on_device
    return body(window_data, factor_one, factor_two, factor_three)


def solution(mesh):
    return jax.shard_map(
        functools.partial(program, mesh.shape["wide"], mesh.shape["narrow"]),
        mesh=mesh,
        in_specs=(
            P(("win", "wide"), "narrow", None),
            P(("win", "narrow"), None),
            P("win", None),
            P(("win", "wide"), None),
        ),
        out_specs=(
            P(("win", "narrow"), None),
            P("win", None),
            P(("win", "wide"), None),
            P(None, ("win", "wide", "narrow")),
        ),
        check_vma=False,
    )
```

```python
import functools

import jax
import jax.numpy as jnp
from jax import lax
from jax.experimental import pallas as pl
from jax.experimental.pallas import tpu as pltpu
from jax.sharding import PartitionSpec as P

highest = lax.Precision.HIGHEST
vmem = pl.BlockSpec(memory_space=pltpu.VMEM)


def contract(form, left, right):
    return jnp.einsum(form, left, right, precision=highest)


def contract_high(form, left, right):
    return jnp.einsum(form, left, right, precision=lax.Precision.HIGH)


def dot(left, right):
    return jnp.dot(left, right, precision=highest, preferred_element_type=jnp.float32)


def dot_t(left, right):
    return lax.dot_general(
        left, right, (((0,), (0,)), ((), ())), precision=highest, preferred_element_type=jnp.float32
    )


def dot_rt(left, right):
    return lax.dot_general(
        left, right, (((1,), (1,)), ((), ())), precision=highest, preferred_element_type=jnp.float32
    )


def inverse_lower(gram):
    rank = gram.shape[0]
    group = 8
    rows = lax.broadcasted_iota(jnp.int32, (rank, rank), 0)
    columns = lax.broadcasted_iota(jnp.int32, (rank, rank), 1)
    both = jnp.concatenate([gram, (rows == columns).astype(jnp.float32)], axis=1)
    blocks = [both[at : at + group] for at in range(0, rank, group)]
    inside = lax.broadcasted_iota(jnp.int32, (group, 2 * rank), 0)
    scales = []
    for step in range(rank):
        at, row = divmod(step, group)
        pivot_row = blocks[at][row : row + 1]
        pivot = pivot_row[:, step : step + 1]
        scales.append(lax.rsqrt(pivot))
        scaled = pivot_row * (1.0 / pivot)
        for later in range(at, rank // group):
            change = blocks[later][:, step : step + 1] * scaled
            if later == at:
                change = jnp.where(inside > row, change, 0.0)
            blocks[later] = blocks[later] - change
    right = jnp.concatenate(blocks, axis=0)[:, rank:]
    return right * jnp.concatenate(scales, axis=0)


class Link:
    def __init__(self, wide, narrow, send, recv):
        self.wide, self.narrow = wide, narrow
        self.send, self.recv = send, recv
        self.used = 0
        self.started = []
        self.w = lax.axis_index("wide")
        self.n = lax.axis_index("narrow")

    def others(self):
        for step in range(1, self.wide * self.narrow):
            dw, dn = divmod(step, self.narrow)
            yield lax.rem(self.w + dw, self.wide), lax.rem(self.n + dn, self.narrow)

    def greet(self):
        barrier = pltpu.get_barrier_semaphore()
        for w, n in self.others():
            pl.semaphore_signal(
                barrier, inc=1, device_id={"wide": w, "narrow": n}, device_id_type=pl.DeviceIdType.MESH
            )
        pl.semaphore_wait(barrier, self.wide * self.narrow - 1)

    def put(self, source, target, w, n):
        copy = pltpu.make_async_remote_copy(
            src_ref=source,
            dst_ref=target,
            send_sem=self.send.at[self.used],
            recv_sem=self.recv.at[self.used],
            device_id={"wide": w, "narrow": n},
            device_id_type=pl.DeviceIdType.MESH,
        )
        self.used += 1
        copy.start()
        self.started.append(copy)
        return copy

    def along_wide(self):
        return [(step, lax.rem(self.w + step, self.wide)) for step in range(1, self.wide)]

    def close(self):
        for copy in self.started:
            copy.wait_send()


def mode_one_kernel(wide, narrow, u_ref, f_ref, basis_ref, core_ref,
                    parts, total, w_send, w_recv, p_send, p_recv, p_all, c_part, c_recv, c_all, send, recv):
    link = Link(wide, narrow, send, recv)
    share = total.shape[1]
    rows = f_ref.shape[0]
    rank = f_ref.shape[1]
    per = rank // wide
    chunk = rows // wide
    half = rank // narrow
    link.greet()
    partner = lax.rem(link.n + 1, narrow)
    copies = []
    for step, w in link.along_wide():
        columns = pl.ds(pl.multiple_of(w * share, 128), share)
        copies.append(link.put(u_ref.at[:, columns], parts.at[step - 1], w, link.n))
    added = u_ref[:, pl.ds(pl.multiple_of(link.w * share, 128), share)]
    for step, copy in enumerate(copies):
        copy.wait_recv()
        added = added + parts[step]
    total[...] = added
    factor = f_ref[...]
    for v in range(per):
        w_send[v] = dot(total[:, v * rows : (v + 1) * rows], factor)
    copy = link.put(w_send, w_recv, link.w, partner)
    copy.wait_recv()
    product = jnp.zeros((rows, rank), jnp.float32)
    for v in range(per):
        product = product + dot_t(total[:, v * rows : (v + 1) * rows], w_send[v] + w_recv[v])
    for w in range(wide):
        p_send[w] = product[w * chunk : (w + 1) * chunk]
    copies = [link.put(p_send.at[w], p_recv.at[step - 1], w, link.n) for step, w in link.along_wide()]
    added = p_send[link.w]
    for step, copy in enumerate(copies):
        copy.wait_recv()
        added = added + p_recv[step]
    mine = link.n * wide + link.w
    p_all[mine] = added
    copies = [link.put(p_all.at[mine], p_all.at[mine], w, n) for w, n in link.others()]
    for copy in copies:
        copy.wait_recv()
    whole = p_all[...].reshape(narrow * rows, rank)
    inverse = inverse_lower(dot_t(whole, whole))
    basis = dot_rt(p_all[pl.ds(link.n * wide, wide)].reshape(rows, rank), inverse)
    basis_ref[...] = basis
    for v in range(per):
        c_part[:, v * rank : (v + 1) * rank] = dot(total[:, v * rows : (v + 1) * rows], basis)
    theirs = pl.ds(pl.multiple_of(partner * half, 8), half)
    copy = link.put(c_part.at[theirs, :], c_recv, link.w, partner)
    own = c_part[pl.ds(pl.multiple_of(link.n * half, 8), half), :]
    copy.wait_recv()
    c_all[link.w, link.n] = own + c_recv[...]
    block = c_all.at[link.w, link.n]
    copies = [link.put(block, block, w, link.n) for _, w in link.along_wide()]
    passed = [link.put(block, block, link.w, partner)]
    for (step, _), copy in zip(link.along_wide(), copies):
        copy.wait_recv()
        source = lax.rem(link.w + wide - step, wide)
        block = c_all.at[source, link.n]
        passed.append(link.put(block, block, link.w, partner))
    for copy in passed:
        copy.wait_recv()
    for w in range(wide):
        for n in range(narrow):
            core_ref[w, n * half : (n + 1) * half] = c_all[w, n]
    link.close()


def mode_two_kernel(wide, narrow, p_ref, basis_ref, p_recv, p_all, send, recv):
    link = Link(wide, narrow, send, recv)
    group = wide * narrow
    link.greet()
    copies = [
        link.put(p_ref.at[w * narrow + n], p_recv.at[step], w, n)
        for step, (w, n) in enumerate(link.others())
    ]
    mine = link.w * narrow + link.n
    added = p_ref[mine]
    for step, copy in enumerate(copies):
        copy.wait_recv()
        added = added + p_recv[step]
    p_all[mine] = added
    copies = [link.put(p_all.at[mine], p_all.at[mine], w, n) for w, n in link.others()]
    for copy in copies:
        copy.wait_recv()
    whole = p_all[...].reshape(basis_ref.shape)
    basis_ref[...] = dot_rt(whole, inverse_lower(dot_t(whole, whole)))
    link.close()


def mode_three_kernel(wide, narrow, u_ref, basis_ref, core_ref, u_all, p_send, p_recv, p_all, send, recv):
    link = Link(wide, narrow, send, recv)
    group = wide * narrow
    rows, rank = basis_ref.shape
    share = core_ref.shape[0]
    link.greet()
    copies = [
        link.put(u_ref.at[w * narrow + n], u_all.at[link.n, link.w], w, n) for w, n in link.others()
    ]
    u_all[link.n, link.w] = u_ref[link.w * narrow + link.n]
    for copy in copies:
        copy.wait_recv()
    factor = u_all[0, :, :, share:].reshape(wide * rows, rank)
    unfold = u_all[0, :, :, :share]
    for n in range(1, narrow):
        unfold = unfold + u_all[n, :, :, :share]
    unfold = unfold.reshape(wide * rows, share)
    product = dot(unfold, dot_t(unfold, factor))
    p_send[...] = product.reshape(wide, rows, rank)
    copies = [link.put(p_send.at[w], p_recv.at[step - 1], w, link.n) for step, w in link.along_wide()]
    added = p_send[link.w]
    for step, copy in enumerate(copies):
        copy.wait_recv()
        added = added + p_recv[step]
    p_all[link.n, link.w] = added
    block = p_all.at[link.n, link.w]
    copies = [link.put(block, block, w, n) for w, n in link.others()]
    for copy in copies:
        copy.wait_recv()
    whole = p_all[0]
    for n in range(1, narrow):
        whole = whole + p_all[n]
    p_recv[...] = whole
    whole = whole.reshape(wide * rows, rank)
    inverse = inverse_lower(dot_t(whole, whole))
    basis_ref[...] = dot_rt(p_recv[link.w], inverse)
    core_ref[...] = dot_t(unfold, dot_rt(whole, inverse))
    link.close()


def call(kernel, wide, narrow, outs, scratch, copies, at, operands):
    return pl.pallas_call(
        functools.partial(kernel, wide, narrow),
        out_shape=[jax.ShapeDtypeStruct(shape, jnp.float32) for shape in outs],
        in_specs=[vmem] * len(operands),
        out_specs=[vmem] * len(outs),
        scratch_shapes=[pltpu.VMEM(shape, jnp.float32) for shape in scratch]
        + [pltpu.SemaphoreType.DMA((copies,))] * 2,
        compiler_params=pltpu.CompilerParams(
            collective_id=at, has_side_effects=True, vmem_limit_bytes=32 * 1024 * 1024
        ),
    )(*operands)


def on_device(wide, narrow, window_data, factor_one, factor_two, factor_three):
    layers, rows, cells = window_data.shape
    rank = factor_one.shape[1]
    group = wide * narrow
    per = rank // wide
    share = per * rows
    along_two = contract_high("kij,jb->kbi", window_data, factor_two).reshape(layers, rank * rows)
    unfold_one = contract_high("kc,kn->cn", factor_three, along_two)
    basis_one, core_two = call(
        mode_one_kernel, wide, narrow,
        [(rows, rank), (wide, rank, per * rank)],
        [
            (wide - 1, rank, share), (rank, share),
            (per, rank, rank), (per, rank, rank),
            (wide, rows // wide, rank), (wide - 1, rows // wide, rank), (group, rows // wide, rank),
            (rank, per * rank), (rank // narrow, per * rank), (wide, narrow, rank // narrow, per * rank),
        ],
        4 * (wide - 1) + 3 + group - 1, 0, (unfold_one, factor_one),
    )
    core_two = core_two.reshape(wide, rank, per, rank)
    along_one = contract_high("kij,ia->kaj", window_data, basis_one)
    spread_two = contract_high("wcva,kc->kawv", core_two, factor_three).reshape(layers, rank, rank)
    product_two = contract_high("kaj,kab->jb", along_one, spread_two)
    basis_two, = call(
        mode_two_kernel, wide, narrow,
        [(cells, rank)],
        [(group - 1, cells // group, rank), (group, cells // group, rank)],
        2 * (group - 1), 1, (product_two.reshape(group, cells // group, rank),),
    )
    along_new = contract_high("kij,jb->kib", window_data, basis_two)
    unfold_three = contract_high("kib,ia->kba", along_new, basis_one)
    shares = rank // group * rank
    unfold_three = unfold_three.reshape(layers, group, shares)
    unfold_three = jnp.concatenate(
        [unfold_three, jnp.broadcast_to(factor_three[:, None], (layers, group, rank))], axis=2
    ).transpose(1, 0, 2)
    basis_three, core = call(
        mode_three_kernel, wide, narrow,
        [(layers, rank), (shares, rank)],
        [
            (narrow, wide, layers, shares + rank),
            (wide, layers, rank), (wide, layers, rank), (narrow, wide, layers, rank),
        ],
        2 * (group - 1) + wide - 1, 2, (unfold_three,),
    )
    core = core.reshape(rank // group, rank, rank).transpose(1, 0, 2).reshape(rank, shares)
    return basis_one, basis_two, basis_three, core


def orthonormal(basis, gram):
    lower = jnp.linalg.cholesky(gram)
    return lax.linalg.triangular_solve(lower, basis, left_side=False, lower=True, transpose_a=True)


def full_core(partial_value):
    flat = partial_value.reshape(
        partial_value.shape[0], partial_value.shape[1] * partial_value.shape[2]
    )
    shares = lax.psum_scatter(flat, ("wide", "narrow"), scatter_dimension=1, tiled=True)
    whole = lax.all_gather(shares, ("wide", "narrow"), axis=1, tiled=True)
    return whole.reshape(partial_value.shape)


def plain_on_device(window_data, factor_one, factor_two, factor_three):
    rank = factor_one.shape[1]
    along_two = contract("kij,jb->kib", window_data, factor_two)
    unfold_part = contract("kib,kc->ibc", along_two, factor_three).reshape(
        along_two.shape[1], rank * rank
    )
    unfold_rows = lax.psum_scatter(unfold_part, "wide", scatter_dimension=1, tiled=True)
    weights_one = lax.psum(jnp.dot(unfold_rows.T, factor_one, precision=highest), "narrow")
    product_one = lax.psum(jnp.dot(unfold_rows, weights_one, precision=highest), "wide")
    gram_one = lax.psum(jnp.dot(product_one.T, product_one, precision=highest), "narrow")
    basis_one = orthonormal(product_one, gram_one)
    along_one = contract("kij,ia->kaj", window_data, basis_one)
    core_two = full_core(
        contract("kab,kc->abc", contract("kaj,jb->kab", along_one, factor_two), factor_three)
    )
    spread_two = contract("abc,kc->kab", core_two, factor_three)
    product_two = lax.psum(contract("kaj,kab->jb", along_one, spread_two), ("wide", "narrow"))
    basis_two = orthonormal(product_two, jnp.dot(product_two.T, product_two, precision=highest))
    along_new = contract("kij,jb->kib", window_data, basis_two)
    unfold_three = contract("kib,ia->kab", along_new, basis_one)
    core_three = full_core(contract("kab,kc->abc", unfold_three, factor_three))
    product_three = lax.psum(contract("kab,abc->kc", unfold_three, core_three), "narrow")
    gram_three = lax.psum(jnp.dot(product_three.T, product_three, precision=highest), "wide")
    basis_three = orthonormal(product_three, gram_three)
    core_part = contract("kab,kc->abc", unfold_three, basis_three).reshape(rank, rank * rank)
    core_shares = lax.psum_scatter(core_part, ("wide", "narrow"), scatter_dimension=1, tiled=True)
    return (basis_one, basis_two, basis_three, core_shares)


def program(wide, narrow, window_data, factor_one, factor_two, factor_three):
    layers, rows, cells = window_data.shape
    rank = factor_one.shape[1]
    group = wide * narrow
    even = (
        narrow == 2
        and rank % (8 * narrow) == 0
        and rank % group == 0
        and (rank // wide * rows) % 128 == 0
        and rows % (8 * wide) == 0
        and cells % (8 * group) == 0
        and layers % 8 == 0
    )
    body = functools.partial(on_device, wide, narrow) if even else plain_on_device
    return body(window_data, factor_one, factor_two, factor_three)


def solution(mesh):
    return jax.shard_map(
        functools.partial(program, mesh.shape["wide"], mesh.shape["narrow"]),
        mesh=mesh,
        in_specs=(
            P(("win", "wide"), "narrow", None),
            P(("win", "narrow"), None),
            P("win", None),
            P(("win", "wide"), None),
        ),
        out_specs=(
            P(("win", "narrow"), None),
            P("win", None),
            P(("win", "wide"), None),
            P(None, ("win", "wide", "narrow")),
        ),
        check_vma=False,
    )
```

```python
import functools

import jax
import jax.numpy as jnp
from jax import lax
from jax.experimental import pallas as pl
from jax.experimental.pallas import tpu as pltpu
from jax.sharding import PartitionSpec as P

highest = lax.Precision.HIGHEST
vmem = pl.BlockSpec(memory_space=pltpu.VMEM)


def contract(form, left, right):
    return jnp.einsum(form, left, right, precision=highest)


def contract_high(form, left, right):
    return jnp.einsum(form, left, right, precision=lax.Precision.HIGH)


def dot(left, right):
    return jnp.dot(left, right, precision=highest, preferred_element_type=jnp.float32)


def dot_t(left, right):
    return lax.dot_general(
        left, right, (((0,), (0,)), ((), ())), precision=highest, preferred_element_type=jnp.float32
    )


def dot_rt(left, right):
    return lax.dot_general(
        left, right, (((1,), (1,)), ((), ())), precision=highest, preferred_element_type=jnp.float32
    )


def inverse_lower(gram):
    rank = gram.shape[0]
    group = 8
    rows = lax.broadcasted_iota(jnp.int32, (rank, rank), 0)
    columns = lax.broadcasted_iota(jnp.int32, (rank, rank), 1)
    both = jnp.concatenate([gram, (rows == columns).astype(jnp.float32)], axis=1)
    blocks = [both[at : at + group] for at in range(0, rank, group)]
    inside = lax.broadcasted_iota(jnp.int32, (group, 2 * rank), 0)
    scales = []
    for step in range(rank):
        at, row = divmod(step, group)
        pivot_row = blocks[at][row : row + 1]
        pivot = pivot_row[:, step : step + 1]
        scales.append(lax.rsqrt(pivot))
        scaled = pivot_row * (1.0 / pivot)
        for later in range(at, rank // group):
            change = blocks[later][:, step : step + 1] * scaled
            if later == at:
                change = jnp.where(inside > row, change, 0.0)
            blocks[later] = blocks[later] - change
    right = jnp.concatenate(blocks, axis=0)[:, rank:]
    return right * jnp.concatenate(scales, axis=0)


class Link:
    def __init__(self, wide, narrow, send, recv):
        self.wide, self.narrow = wide, narrow
        self.send, self.recv = send, recv
        self.used = 0
        self.started = []
        self.w = lax.axis_index("wide")
        self.n = lax.axis_index("narrow")

    def others(self):
        for step in range(1, self.wide * self.narrow):
            dw, dn = divmod(step, self.narrow)
            yield lax.rem(self.w + dw, self.wide), lax.rem(self.n + dn, self.narrow)

    def greet(self):
        barrier = pltpu.get_barrier_semaphore()
        for w, n in self.others():
            pl.semaphore_signal(
                barrier, inc=1, device_id={"wide": w, "narrow": n}, device_id_type=pl.DeviceIdType.MESH
            )
        pl.semaphore_wait(barrier, self.wide * self.narrow - 1)

    def put(self, source, target, w, n):
        copy = pltpu.make_async_remote_copy(
            src_ref=source,
            dst_ref=target,
            send_sem=self.send.at[self.used],
            recv_sem=self.recv.at[self.used],
            device_id={"wide": w, "narrow": n},
            device_id_type=pl.DeviceIdType.MESH,
        )
        self.used += 1
        copy.start()
        self.started.append(copy)
        return copy

    def along_wide(self):
        return [(step, lax.rem(self.w + step, self.wide)) for step in range(1, self.wide)]

    def close(self):
        for copy in self.started:
            copy.wait_send()


def mode_one_kernel(wide, narrow, u_ref, f_ref, basis_ref, core_ref,
                    parts, total, w_send, w_recv, p_send, p_recv, p_all, c_part, c_recv, c_all, send, recv):
    link = Link(wide, narrow, send, recv)
    share = total.shape[1]
    rows = f_ref.shape[0]
    rank = f_ref.shape[1]
    per = rank // wide
    chunk = rows // wide
    half = rank // narrow
    link.greet()
    partner = lax.rem(link.n + 1, narrow)
    copies = []
    for step, w in link.along_wide():
        columns = pl.ds(pl.multiple_of(w * share, 128), share)
        copies.append(link.put(u_ref.at[:, columns], parts.at[step - 1], w, link.n))
    added = u_ref[:, pl.ds(pl.multiple_of(link.w * share, 128), share)]
    for step, copy in enumerate(copies):
        copy.wait_recv()
        added = added + parts[step]
    total[...] = added
    factor = f_ref[...]
    for v in range(per):
        w_send[v] = dot(total[:, v * rows : (v + 1) * rows], factor)
    copy = link.put(w_send, w_recv, link.w, partner)
    copy.wait_recv()
    product = jnp.zeros((rows, rank), jnp.float32)
    for v in range(per):
        product = product + dot_t(total[:, v * rows : (v + 1) * rows], w_send[v] + w_recv[v])
    for w in range(wide):
        p_send[w] = product[w * chunk : (w + 1) * chunk]
    copies = [link.put(p_send.at[w], p_recv.at[step - 1], w, link.n) for step, w in link.along_wide()]
    added = p_send[link.w]
    for step, copy in enumerate(copies):
        copy.wait_recv()
        added = added + p_recv[step]
    mine = link.n * wide + link.w
    p_all[mine] = added
    copies = [link.put(p_all.at[mine], p_all.at[mine], w, n) for w, n in link.others()]
    for copy in copies:
        copy.wait_recv()
    whole = p_all[...].reshape(narrow * rows, rank)
    inverse = inverse_lower(dot_t(whole, whole))
    basis = dot_rt(p_all[pl.ds(link.n * wide, wide)].reshape(rows, rank), inverse)
    basis_ref[...] = basis
    for v in range(per):
        c_part[:, v * rank : (v + 1) * rank] = dot(total[:, v * rows : (v + 1) * rows], basis)
    theirs = pl.ds(pl.multiple_of(partner * half, 8), half)
    copy = link.put(c_part.at[theirs, :], c_recv, link.w, partner)
    own = c_part[pl.ds(pl.multiple_of(link.n * half, 8), half), :]
    copy.wait_recv()
    c_all[link.w, link.n] = own + c_recv[...]
    block = c_all.at[link.w, link.n]
    copies = [link.put(block, block, w, link.n) for _, w in link.along_wide()]
    passed = [link.put(block, block, link.w, partner)]
    for (step, _), copy in zip(link.along_wide(), copies):
        copy.wait_recv()
        source = lax.rem(link.w + wide - step, wide)
        block = c_all.at[source, link.n]
        passed.append(link.put(block, block, link.w, partner))
    for copy in passed:
        copy.wait_recv()
    for w in range(wide):
        for n in range(narrow):
            core_ref[w, n * half : (n + 1) * half] = c_all[w, n]
    link.close()


def mode_two_kernel(wide, narrow, p_ref, basis_ref, p_recv, p_all, send, recv):
    link = Link(wide, narrow, send, recv)
    group = wide * narrow
    link.greet()
    copies = [
        link.put(p_ref.at[w * narrow + n], p_recv.at[step], w, n)
        for step, (w, n) in enumerate(link.others())
    ]
    mine = link.w * narrow + link.n
    added = p_ref[mine]
    for step, copy in enumerate(copies):
        copy.wait_recv()
        added = added + p_recv[step]
    p_all[mine] = added
    copies = [link.put(p_all.at[mine], p_all.at[mine], w, n) for w, n in link.others()]
    for copy in copies:
        copy.wait_recv()
    whole = p_all[...].reshape(basis_ref.shape)
    basis_ref[...] = dot_rt(whole, inverse_lower(dot_t(whole, whole)))
    link.close()


def mode_three_kernel(wide, narrow, u_ref, basis_ref, core_ref, u_all, p_send, p_recv, p_all, send, recv):
    link = Link(wide, narrow, send, recv)
    group = wide * narrow
    rows, rank = basis_ref.shape
    share = core_ref.shape[0]
    link.greet()
    copies = [
        link.put(u_ref.at[w * narrow + n], u_all.at[link.n, link.w], w, n) for w, n in link.others()
    ]
    u_all[link.n, link.w] = u_ref[link.w * narrow + link.n]
    for copy in copies:
        copy.wait_recv()
    factor = u_all[0, :, :, share:].reshape(wide * rows, rank)
    unfold = u_all[0, :, :, :share]
    for n in range(1, narrow):
        unfold = unfold + u_all[n, :, :, :share]
    unfold = unfold.reshape(wide * rows, share)
    product = dot(unfold, dot_t(unfold, factor))
    p_send[...] = product.reshape(wide, rows, rank)
    copies = [link.put(p_send.at[w], p_recv.at[step - 1], w, link.n) for step, w in link.along_wide()]
    added = p_send[link.w]
    for step, copy in enumerate(copies):
        copy.wait_recv()
        added = added + p_recv[step]
    p_all[link.n, link.w] = added
    block = p_all.at[link.n, link.w]
    copies = [link.put(block, block, w, n) for w, n in link.others()]
    for copy in copies:
        copy.wait_recv()
    whole = p_all[0]
    for n in range(1, narrow):
        whole = whole + p_all[n]
    p_recv[...] = whole
    whole = whole.reshape(wide * rows, rank)
    inverse = inverse_lower(dot_t(whole, whole))
    basis_ref[...] = dot_rt(p_recv[link.w], inverse)
    core_ref[...] = dot_t(unfold, dot_rt(whole, inverse))
    link.close()


def call(kernel, wide, narrow, outs, scratch, copies, at, operands):
    return pl.pallas_call(
        functools.partial(kernel, wide, narrow),
        out_shape=[jax.ShapeDtypeStruct(shape, jnp.float32) for shape in outs],
        in_specs=[vmem] * len(operands),
        out_specs=[vmem] * len(outs),
        scratch_shapes=[pltpu.VMEM(shape, jnp.float32) for shape in scratch]
        + [pltpu.SemaphoreType.DMA((copies,))] * 2,
        compiler_params=pltpu.CompilerParams(
            collective_id=at, has_side_effects=True, vmem_limit_bytes=32 * 1024 * 1024
        ),
    )(*operands)


def on_device(wide, narrow, window_data, factor_one, factor_two, factor_three):
    layers, rows, cells = window_data.shape
    rank = factor_one.shape[1]
    group = wide * narrow
    per = rank // wide
    share = per * rows
    along_two = contract_high("kij,jb->kbi", window_data, factor_two).reshape(layers, rank * rows)
    unfold_one = contract_high("kc,kn->cn", factor_three, along_two)
    basis_one, core_two = call(
        mode_one_kernel, wide, narrow,
        [(rows, rank), (wide, rank, per * rank)],
        [
            (wide - 1, rank, share), (rank, share),
            (per, rank, rank), (per, rank, rank),
            (wide, rows // wide, rank), (wide - 1, rows // wide, rank), (group, rows // wide, rank),
            (rank, per * rank), (rank // narrow, per * rank), (wide, narrow, rank // narrow, per * rank),
        ],
        4 * (wide - 1) + 3 + group - 1, 0, (unfold_one, factor_one),
    )
    core_two = core_two.reshape(wide, rank, per, rank)
    along_one = contract_high("kij,ia->akj", window_data, basis_one)
    spread_two = contract_high("wcva,kc->akwv", core_two, factor_three).reshape(rank, layers, rank)
    product_two = contract_high("akj,akb->jb", along_one, spread_two)
    basis_two, = call(
        mode_two_kernel, wide, narrow,
        [(cells, rank)],
        [(group - 1, cells // group, rank), (group, cells // group, rank)],
        2 * (group - 1), 1, (product_two.reshape(group, cells // group, rank),),
    )
    along_new = contract_high("kij,jb->kib", window_data, basis_two)
    unfold_three = contract_high("kib,ia->kba", along_new, basis_one)
    shares = rank // group * rank
    unfold_three = unfold_three.reshape(layers, group, shares)
    unfold_three = jnp.concatenate(
        [unfold_three, jnp.broadcast_to(factor_three[:, None], (layers, group, rank))], axis=2
    ).transpose(1, 0, 2)
    basis_three, core = call(
        mode_three_kernel, wide, narrow,
        [(layers, rank), (shares, rank)],
        [
            (narrow, wide, layers, shares + rank),
            (wide, layers, rank), (wide, layers, rank), (narrow, wide, layers, rank),
        ],
        2 * (group - 1) + wide - 1, 2, (unfold_three,),
    )
    core = core.reshape(rank // group, rank, rank).transpose(1, 0, 2).reshape(rank, shares)
    return basis_one, basis_two, basis_three, core


def orthonormal(basis, gram):
    lower = jnp.linalg.cholesky(gram)
    return lax.linalg.triangular_solve(lower, basis, left_side=False, lower=True, transpose_a=True)


def full_core(partial_value):
    flat = partial_value.reshape(
        partial_value.shape[0], partial_value.shape[1] * partial_value.shape[2]
    )
    shares = lax.psum_scatter(flat, ("wide", "narrow"), scatter_dimension=1, tiled=True)
    whole = lax.all_gather(shares, ("wide", "narrow"), axis=1, tiled=True)
    return whole.reshape(partial_value.shape)


def plain_on_device(window_data, factor_one, factor_two, factor_three):
    rank = factor_one.shape[1]
    along_two = contract("kij,jb->kib", window_data, factor_two)
    unfold_part = contract("kib,kc->ibc", along_two, factor_three).reshape(
        along_two.shape[1], rank * rank
    )
    unfold_rows = lax.psum_scatter(unfold_part, "wide", scatter_dimension=1, tiled=True)
    weights_one = lax.psum(jnp.dot(unfold_rows.T, factor_one, precision=highest), "narrow")
    product_one = lax.psum(jnp.dot(unfold_rows, weights_one, precision=highest), "wide")
    gram_one = lax.psum(jnp.dot(product_one.T, product_one, precision=highest), "narrow")
    basis_one = orthonormal(product_one, gram_one)
    along_one = contract("kij,ia->kaj", window_data, basis_one)
    core_two = full_core(
        contract("kab,kc->abc", contract("kaj,jb->kab", along_one, factor_two), factor_three)
    )
    spread_two = contract("abc,kc->kab", core_two, factor_three)
    product_two = lax.psum(contract("kaj,kab->jb", along_one, spread_two), ("wide", "narrow"))
    basis_two = orthonormal(product_two, jnp.dot(product_two.T, product_two, precision=highest))
    along_new = contract("kij,jb->kib", window_data, basis_two)
    unfold_three = contract("kib,ia->kab", along_new, basis_one)
    core_three = full_core(contract("kab,kc->abc", unfold_three, factor_three))
    product_three = lax.psum(contract("kab,abc->kc", unfold_three, core_three), "narrow")
    gram_three = lax.psum(jnp.dot(product_three.T, product_three, precision=highest), "wide")
    basis_three = orthonormal(product_three, gram_three)
    core_part = contract("kab,kc->abc", unfold_three, basis_three).reshape(rank, rank * rank)
    core_shares = lax.psum_scatter(core_part, ("wide", "narrow"), scatter_dimension=1, tiled=True)
    return (basis_one, basis_two, basis_three, core_shares)


def program(wide, narrow, window_data, factor_one, factor_two, factor_three):
    layers, rows, cells = window_data.shape
    rank = factor_one.shape[1]
    group = wide * narrow
    even = (
        narrow == 2
        and rank % (8 * narrow) == 0
        and rank % group == 0
        and (rank // wide * rows) % 128 == 0
        and rows % (8 * wide) == 0
        and cells % (8 * group) == 0
        and layers % 8 == 0
    )
    body = functools.partial(on_device, wide, narrow) if even else plain_on_device
    return body(window_data, factor_one, factor_two, factor_three)


def solution(mesh):
    return jax.shard_map(
        functools.partial(program, mesh.shape["wide"], mesh.shape["narrow"]),
        mesh=mesh,
        in_specs=(
            P(("win", "wide"), "narrow", None),
            P(("win", "narrow"), None),
            P("win", None),
            P(("win", "wide"), None),
        ),
        out_specs=(
            P(("win", "narrow"), None),
            P("win", None),
            P(("win", "wide"), None),
            P(None, ("win", "wide", "narrow")),
        ),
        check_vma=False,
    )
```

```python
import functools

import jax
import jax.numpy as jnp
from jax import lax
from jax.experimental import pallas as pl
from jax.experimental.pallas import tpu as pltpu
from jax.sharding import PartitionSpec as P

highest = lax.Precision.HIGHEST
vmem = pl.BlockSpec(memory_space=pltpu.VMEM)


def contract(form, left, right):
    return jnp.einsum(form, left, right, precision=highest)


def contract_high(form, left, right):
    return jnp.einsum(form, left, right, precision=lax.Precision.HIGH)


def dot(left, right):
    return jnp.dot(left, right, precision=highest, preferred_element_type=jnp.float32)


def dot_t(left, right):
    return lax.dot_general(
        left, right, (((0,), (0,)), ((), ())), precision=highest, preferred_element_type=jnp.float32
    )


def dot_rt(left, right):
    return lax.dot_general(
        left, right, (((1,), (1,)), ((), ())), precision=highest, preferred_element_type=jnp.float32
    )


def inverse_lower(gram):
    rank = gram.shape[0]
    group = 8
    rows = lax.broadcasted_iota(jnp.int32, (rank, rank), 0)
    columns = lax.broadcasted_iota(jnp.int32, (rank, rank), 1)
    both = jnp.concatenate([gram, (rows == columns).astype(jnp.float32)], axis=1)
    blocks = [both[at : at + group] for at in range(0, rank, group)]
    inside = lax.broadcasted_iota(jnp.int32, (group, 2 * rank), 0)
    pivots = [jnp.ones((group, 2 * rank), jnp.float32) for _ in blocks]
    for step in range(rank):
        at, row = divmod(step, group)
        column = jnp.broadcast_to(blocks[at][:, step : step + 1], (group, 2 * rank))
        pivot = column[row : row + 1]
        pivots[at] = jnp.where(inside == row, pivot, pivots[at])
        scaled = blocks[at][row : row + 1] * (1.0 / pivot)
        blocks[at] = blocks[at] - jnp.where(inside > row, column * scaled, 0.0)
        for later in range(at + 1, rank // group):
            blocks[later] = blocks[later] - blocks[later][:, step : step + 1] * scaled
    blocks = [block * lax.rsqrt(pivot) for block, pivot in zip(blocks, pivots)]
    return jnp.concatenate(blocks, axis=0)[:, rank:]


class Link:
    def __init__(self, wide, narrow, send, recv):
        self.wide, self.narrow = wide, narrow
        self.send, self.recv = send, recv
        self.used = 0
        self.started = []
        self.w = lax.axis_index("wide")
        self.n = lax.axis_index("narrow")

    def others(self):
        for step in range(1, self.wide * self.narrow):
            dw, dn = divmod(step, self.narrow)
            yield lax.rem(self.w + dw, self.wide), lax.rem(self.n + dn, self.narrow)

    def greet(self):
        barrier = pltpu.get_barrier_semaphore()
        for w, n in self.others():
            pl.semaphore_signal(
                barrier, inc=1, device_id={"wide": w, "narrow": n}, device_id_type=pl.DeviceIdType.MESH
            )
        pl.semaphore_wait(barrier, self.wide * self.narrow - 1)

    def put(self, source, target, w, n):
        copy = pltpu.make_async_remote_copy(
            src_ref=source,
            dst_ref=target,
            send_sem=self.send.at[self.used],
            recv_sem=self.recv.at[self.used],
            device_id={"wide": w, "narrow": n},
            device_id_type=pl.DeviceIdType.MESH,
        )
        self.used += 1
        copy.start()
        self.started.append(copy)
        return copy

    def along_wide(self):
        return [(step, lax.rem(self.w + step, self.wide)) for step in range(1, self.wide)]

    def close(self):
        for copy in self.started:
            copy.wait_send()


def mode_one_kernel(wide, narrow, u_ref, f_ref, basis_ref, dual_ref, core_ref,
                    parts, total, w_send, w_recv, p_send, p_recv, p_all, c_part, c_recv, c_all, send, recv):
    link = Link(wide, narrow, send, recv)
    share = total.shape[1]
    rows = f_ref.shape[0]
    rank = f_ref.shape[1]
    per = rank // wide
    chunk = rows // wide
    half = rank // narrow
    link.greet()
    partner = lax.rem(link.n + 1, narrow)
    copies = []
    for step, w in link.along_wide():
        columns = pl.ds(pl.multiple_of(w * share, 128), share)
        copies.append(link.put(u_ref.at[:, columns], parts.at[step - 1], w, link.n))
    added = u_ref[:, pl.ds(pl.multiple_of(link.w * share, 128), share)]
    for step, copy in enumerate(copies):
        copy.wait_recv()
        added = added + parts[step]
    total[...] = added
    factor = f_ref[...]
    for v in range(per):
        w_send[v] = dot(total[:, v * rows : (v + 1) * rows], factor)
    copy = link.put(w_send, w_recv, link.w, partner)
    copy.wait_recv()
    product = jnp.zeros((rows, rank), jnp.float32)
    for v in range(per):
        product = product + dot_t(total[:, v * rows : (v + 1) * rows], w_send[v] + w_recv[v])
    for w in range(wide):
        p_send[w] = product[w * chunk : (w + 1) * chunk]
    copies = [link.put(p_send.at[w], p_recv.at[step - 1], w, link.n) for step, w in link.along_wide()]
    added = p_send[link.w]
    for step, copy in enumerate(copies):
        copy.wait_recv()
        added = added + p_recv[step]
    mine = link.n * wide + link.w
    p_all[mine] = added
    copies = [link.put(p_all.at[mine], p_all.at[mine], w, n) for w, n in link.others()]
    for copy in copies:
        copy.wait_recv()
    whole = p_all[...].reshape(narrow * rows, rank)
    held = p_all[pl.ds(link.n * wide, wide)].reshape(rows, rank)
    for v in range(per):
        c_part[:, v * rank : (v + 1) * rank] = dot(total[:, v * rows : (v + 1) * rows], held)
    theirs = pl.ds(pl.multiple_of(partner * half, 8), half)
    copy = link.put(c_part.at[theirs, :], c_recv, link.w, partner)
    own = c_part[pl.ds(pl.multiple_of(link.n * half, 8), half), :]
    copy.wait_recv()
    c_all[link.w, link.n] = own + c_recv[...]
    block = c_all.at[link.w, link.n]
    copies = [link.put(block, block, w, link.n) for _, w in link.along_wide()]
    passed = [link.put(block, block, link.w, partner)]
    inverse = inverse_lower(dot_t(whole, whole))
    basis = dot_rt(held, inverse)
    basis_ref[...] = basis
    dual_ref[...] = dot(basis, inverse)
    for (step, _), copy in zip(link.along_wide(), copies):
        copy.wait_recv()
        source = lax.rem(link.w + wide - step, wide)
        block = c_all.at[source, link.n]
        passed.append(link.put(block, block, link.w, partner))
    for copy in passed:
        copy.wait_recv()
    for w in range(wide):
        for n in range(narrow):
            core_ref[w, n * half : (n + 1) * half] = c_all[w, n]
    link.close()


def mode_two_kernel(wide, narrow, p_ref, basis_ref, p_recv, p_all, send, recv):
    link = Link(wide, narrow, send, recv)
    group = wide * narrow
    link.greet()
    copies = [
        link.put(p_ref.at[w * narrow + n], p_recv.at[step], w, n)
        for step, (w, n) in enumerate(link.others())
    ]
    mine = link.w * narrow + link.n
    added = p_ref[mine]
    for step, copy in enumerate(copies):
        copy.wait_recv()
        added = added + p_recv[step]
    p_all[mine] = added
    copies = [link.put(p_all.at[mine], p_all.at[mine], w, n) for w, n in link.others()]
    for copy in copies:
        copy.wait_recv()
    whole = p_all[...].reshape(basis_ref.shape)
    basis_ref[...] = dot_rt(whole, inverse_lower(dot_t(whole, whole)))
    link.close()


def mode_three_kernel(wide, narrow, u_ref, basis_ref, core_ref, u_all, p_send, p_recv, p_all, send, recv):
    link = Link(wide, narrow, send, recv)
    group = wide * narrow
    rows, rank = basis_ref.shape
    share = core_ref.shape[0]
    link.greet()
    copies = [
        link.put(u_ref.at[w * narrow + n], u_all.at[link.n, link.w], w, n) for w, n in link.others()
    ]
    u_all[link.n, link.w] = u_ref[link.w * narrow + link.n]
    for copy in copies:
        copy.wait_recv()
    factor = u_all[0, :, :, share:].reshape(wide * rows, rank)
    unfold = u_all[0, :, :, :share]
    for n in range(1, narrow):
        unfold = unfold + u_all[n, :, :, :share]
    unfold = unfold.reshape(wide * rows, share)
    product = dot(unfold, dot_t(unfold, factor))
    p_send[...] = product.reshape(wide, rows, rank)
    copies = [link.put(p_send.at[w], p_recv.at[step - 1], w, link.n) for step, w in link.along_wide()]
    added = p_send[link.w]
    for step, copy in enumerate(copies):
        copy.wait_recv()
        added = added + p_recv[step]
    p_all[link.n, link.w] = added
    block = p_all.at[link.n, link.w]
    copies = [link.put(block, block, w, n) for w, n in link.others()]
    for copy in copies:
        copy.wait_recv()
    whole = p_all[0]
    for n in range(1, narrow):
        whole = whole + p_all[n]
    p_recv[...] = whole
    whole = whole.reshape(wide * rows, rank)
    inverse = inverse_lower(dot_t(whole, whole))
    basis_ref[...] = dot_rt(p_recv[link.w], inverse)
    core_ref[...] = dot_t(unfold, dot_rt(whole, inverse))
    link.close()


def call(kernel, wide, narrow, outs, scratch, copies, at, operands):
    return pl.pallas_call(
        functools.partial(kernel, wide, narrow),
        out_shape=[jax.ShapeDtypeStruct(shape, jnp.float32) for shape in outs],
        in_specs=[vmem] * len(operands),
        out_specs=[vmem] * len(outs),
        scratch_shapes=[pltpu.VMEM(shape, jnp.float32) for shape in scratch]
        + [pltpu.SemaphoreType.DMA((copies,))] * 2,
        compiler_params=pltpu.CompilerParams(
            collective_id=at, has_side_effects=True, vmem_limit_bytes=32 * 1024 * 1024
        ),
    )(*operands)


def on_device(wide, narrow, window_data, factor_one, factor_two, factor_three):
    layers, rows, cells = window_data.shape
    rank = factor_one.shape[1]
    group = wide * narrow
    per = rank // wide
    share = per * rows
    along_two = contract_high("kij,jb->kbi", window_data, factor_two).reshape(layers, rank * rows)
    unfold_one = contract_high("kc,kn->cn", factor_three, along_two)
    basis_one, dual_one, core_two = call(
        mode_one_kernel, wide, narrow,
        [(rows, rank), (rows, rank), (wide, rank, per * rank)],
        [
            (wide - 1, rank, share), (rank, share),
            (per, rank, rank), (per, rank, rank),
            (wide, rows // wide, rank), (wide - 1, rows // wide, rank), (group, rows // wide, rank),
            (rank, per * rank), (rank // narrow, per * rank), (wide, narrow, rank // narrow, per * rank),
        ],
        4 * (wide - 1) + 3 + group - 1, 0, (unfold_one, factor_one),
    )
    core_two = core_two.reshape(wide, rank, per, rank)
    along_one = contract_high("kij,ia->kaj", window_data, dual_one)
    spread_two = contract_high("wcva,kc->kawv", core_two, factor_three).reshape(layers, rank, rank)
    product_two = contract_high("kaj,kab->jb", along_one, spread_two)
    basis_two, = call(
        mode_two_kernel, wide, narrow,
        [(cells, rank)],
        [(group - 1, cells // group, rank), (group, cells // group, rank)],
        2 * (group - 1), 1, (product_two.reshape(group, cells // group, rank),),
    )
    along_new = contract_high("kij,jb->kib", window_data, basis_two)
    unfold_three = contract_high("kib,ia->kba", along_new, basis_one)
    shares = rank // group * rank
    unfold_three = unfold_three.reshape(layers, group, shares)
    unfold_three = jnp.concatenate(
        [unfold_three, jnp.broadcast_to(factor_three[:, None], (layers, group, rank))], axis=2
    ).transpose(1, 0, 2)
    basis_three, core = call(
        mode_three_kernel, wide, narrow,
        [(layers, rank), (shares, rank)],
        [
            (narrow, wide, layers, shares + rank),
            (wide, layers, rank), (wide, layers, rank), (narrow, wide, layers, rank),
        ],
        2 * (group - 1) + wide - 1, 2, (unfold_three,),
    )
    core = core.reshape(rank // group, rank, rank).transpose(1, 0, 2).reshape(rank, shares)
    return basis_one, basis_two, basis_three, core


def orthonormal(basis, gram):
    lower = jnp.linalg.cholesky(gram)
    return lax.linalg.triangular_solve(lower, basis, left_side=False, lower=True, transpose_a=True)


def full_core(partial_value):
    flat = partial_value.reshape(
        partial_value.shape[0], partial_value.shape[1] * partial_value.shape[2]
    )
    shares = lax.psum_scatter(flat, ("wide", "narrow"), scatter_dimension=1, tiled=True)
    whole = lax.all_gather(shares, ("wide", "narrow"), axis=1, tiled=True)
    return whole.reshape(partial_value.shape)


def plain_on_device(window_data, factor_one, factor_two, factor_three):
    rank = factor_one.shape[1]
    along_two = contract("kij,jb->kib", window_data, factor_two)
    unfold_part = contract("kib,kc->ibc", along_two, factor_three).reshape(
        along_two.shape[1], rank * rank
    )
    unfold_rows = lax.psum_scatter(unfold_part, "wide", scatter_dimension=1, tiled=True)
    weights_one = lax.psum(jnp.dot(unfold_rows.T, factor_one, precision=highest), "narrow")
    product_one = lax.psum(jnp.dot(unfold_rows, weights_one, precision=highest), "wide")
    gram_one = lax.psum(jnp.dot(product_one.T, product_one, precision=highest), "narrow")
    basis_one = orthonormal(product_one, gram_one)
    along_one = contract("kij,ia->kaj", window_data, basis_one)
    core_two = full_core(
        contract("kab,kc->abc", contract("kaj,jb->kab", along_one, factor_two), factor_three)
    )
    spread_two = contract("abc,kc->kab", core_two, factor_three)
    product_two = lax.psum(contract("kaj,kab->jb", along_one, spread_two), ("wide", "narrow"))
    basis_two = orthonormal(product_two, jnp.dot(product_two.T, product_two, precision=highest))
    along_new = contract("kij,jb->kib", window_data, basis_two)
    unfold_three = contract("kib,ia->kab", along_new, basis_one)
    core_three = full_core(contract("kab,kc->abc", unfold_three, factor_three))
    product_three = lax.psum(contract("kab,abc->kc", unfold_three, core_three), "narrow")
    gram_three = lax.psum(jnp.dot(product_three.T, product_three, precision=highest), "wide")
    basis_three = orthonormal(product_three, gram_three)
    core_part = contract("kab,kc->abc", unfold_three, basis_three).reshape(rank, rank * rank)
    core_shares = lax.psum_scatter(core_part, ("wide", "narrow"), scatter_dimension=1, tiled=True)
    return (basis_one, basis_two, basis_three, core_shares)


def program(wide, narrow, window_data, factor_one, factor_two, factor_three):
    layers, rows, cells = window_data.shape
    rank = factor_one.shape[1]
    group = wide * narrow
    even = (
        narrow == 2
        and rank % (8 * narrow) == 0
        and rank % group == 0
        and (rank // wide * rows) % 128 == 0
        and rows % (8 * wide) == 0
        and cells % (8 * group) == 0
        and layers % 8 == 0
    )
    body = functools.partial(on_device, wide, narrow) if even else plain_on_device
    return body(window_data, factor_one, factor_two, factor_three)


def solution(mesh):
    return jax.shard_map(
        functools.partial(program, mesh.shape["wide"], mesh.shape["narrow"]),
        mesh=mesh,
        in_specs=(
            P(("win", "wide"), "narrow", None),
            P(("win", "narrow"), None),
            P("win", None),
            P(("win", "wide"), None),
        ),
        out_specs=(
            P(("win", "narrow"), None),
            P("win", None),
            P(("win", "wide"), None),
            P(None, ("win", "wide", "narrow")),
        ),
        check_vma=False,
    )
```

```python
import functools

import jax
import jax.numpy as jnp
from jax import lax
from jax.experimental import pallas as pl
from jax.experimental.pallas import tpu as pltpu
from jax.sharding import PartitionSpec as P

highest = lax.Precision.HIGHEST
vmem = pl.BlockSpec(memory_space=pltpu.VMEM)


def contract(form, left, right):
    return jnp.einsum(form, left, right, precision=highest)


def contract_high(form, left, right):
    return jnp.einsum(form, left, right, precision=lax.Precision.HIGH)


def dot(left, right):
    return jnp.dot(left, right, precision=highest, preferred_element_type=jnp.float32)


def dot_t(left, right):
    return lax.dot_general(
        left, right, (((0,), (0,)), ((), ())), precision=highest, preferred_element_type=jnp.float32
    )


def dot_rt(left, right):
    return lax.dot_general(
        left, right, (((1,), (1,)), ((), ())), precision=highest, preferred_element_type=jnp.float32
    )


def inverse_lower(gram):
    rank = gram.shape[0]
    group = 8
    rows = lax.broadcasted_iota(jnp.int32, (rank, rank), 0)
    columns = lax.broadcasted_iota(jnp.int32, (rank, rank), 1)
    both = jnp.concatenate([gram, (rows == columns).astype(jnp.float32)], axis=1)
    blocks = [both[at : at + group] for at in range(0, rank, group)]
    inside = lax.broadcasted_iota(jnp.int32, (group, 2 * rank), 0)
    wide_shape = (group, 2 * rank)
    for at in range(rank // group):
        later = range(at, rank // group)
        spread = [
            {k: jnp.broadcast_to(blocks[k][:, at * group + t : at * group + t + 1], wide_shape) for k in later}
            for t in range(group)
        ]
        pivots = jnp.ones(wide_shape, jnp.float32)
        for row in range(group):
            pivot = spread[row][at][row : row + 1]
            pivots = jnp.where(inside == row, pivot, pivots)
            over = 1.0 / pivot
            column = dict(spread[row])
            column[at] = jnp.where(inside > row, column[at], 0.0)
            for t in range(row + 1, group):
                factor = spread[t][at][row : row + 1] * over
                spread[t] = {k: spread[t][k] - column[k] * factor for k in later}
            scaled = blocks[at][row : row + 1] * over
            for k in later:
                blocks[k] = blocks[k] - column[k] * scaled
        blocks[at] = blocks[at] * lax.rsqrt(pivots)
    return jnp.concatenate(blocks, axis=0)[:, rank:]


class Link:
    def __init__(self, wide, narrow, send, recv):
        self.wide, self.narrow = wide, narrow
        self.send, self.recv = send, recv
        self.used = 0
        self.started = []
        self.w = lax.axis_index("wide")
        self.n = lax.axis_index("narrow")

    def others(self):
        for step in range(1, self.wide * self.narrow):
            dw, dn = divmod(step, self.narrow)
            yield lax.rem(self.w + dw, self.wide), lax.rem(self.n + dn, self.narrow)

    def greet(self):
        barrier = pltpu.get_barrier_semaphore()
        for w, n in self.others():
            pl.semaphore_signal(
                barrier, inc=1, device_id={"wide": w, "narrow": n}, device_id_type=pl.DeviceIdType.MESH
            )
        pl.semaphore_wait(barrier, self.wide * self.narrow - 1)

    def put(self, source, target, w, n):
        copy = pltpu.make_async_remote_copy(
            src_ref=source,
            dst_ref=target,
            send_sem=self.send.at[self.used],
            recv_sem=self.recv.at[self.used],
            device_id={"wide": w, "narrow": n},
            device_id_type=pl.DeviceIdType.MESH,
        )
        self.used += 1
        copy.start()
        self.started.append(copy)
        return copy

    def along_wide(self):
        return [(step, lax.rem(self.w + step, self.wide)) for step in range(1, self.wide)]

    def close(self):
        for copy in self.started:
            copy.wait_send()


def mode_one_kernel(wide, narrow, u_ref, f_ref, basis_ref, core_ref,
                    parts, total, w_send, w_recv, p_send, p_recv, p_all, c_part, c_recv, c_all, send, recv):
    link = Link(wide, narrow, send, recv)
    share = total.shape[1]
    rows = f_ref.shape[0]
    rank = f_ref.shape[1]
    per = rank // wide
    chunk = rows // wide
    half = rank // narrow
    link.greet()
    partner = lax.rem(link.n + 1, narrow)
    copies = []
    for step, w in link.along_wide():
        columns = pl.ds(pl.multiple_of(w * share, 128), share)
        copies.append(link.put(u_ref.at[:, columns], parts.at[step - 1], w, link.n))
    added = u_ref[:, pl.ds(pl.multiple_of(link.w * share, 128), share)]
    for step, copy in enumerate(copies):
        copy.wait_recv()
        added = added + parts[step]
    total[...] = added
    factor = f_ref[...]
    for v in range(per):
        w_send[v] = dot(total[:, v * rows : (v + 1) * rows], factor)
    copy = link.put(w_send, w_recv, link.w, partner)
    copy.wait_recv()
    product = jnp.zeros((rows, rank), jnp.float32)
    for v in range(per):
        product = product + dot_t(total[:, v * rows : (v + 1) * rows], w_send[v] + w_recv[v])
    for w in range(wide):
        p_send[w] = product[w * chunk : (w + 1) * chunk]
    copies = [link.put(p_send.at[w], p_recv.at[step - 1], w, link.n) for step, w in link.along_wide()]
    added = p_send[link.w]
    for step, copy in enumerate(copies):
        copy.wait_recv()
        added = added + p_recv[step]
    mine = link.n * wide + link.w
    p_all[mine] = added
    copies = [link.put(p_all.at[mine], p_all.at[mine], w, n) for w, n in link.others()]
    for copy in copies:
        copy.wait_recv()
    whole = p_all[...].reshape(narrow * rows, rank)
    inverse = inverse_lower(dot_t(whole, whole))
    basis = dot_rt(p_all[pl.ds(link.n * wide, wide)].reshape(rows, rank), inverse)
    basis_ref[...] = basis
    for v in range(per):
        c_part[:, v * rank : (v + 1) * rank] = dot(total[:, v * rows : (v + 1) * rows], basis)
    theirs = pl.ds(pl.multiple_of(partner * half, 8), half)
    copy = link.put(c_part.at[theirs, :], c_recv, link.w, partner)
    own = c_part[pl.ds(pl.multiple_of(link.n * half, 8), half), :]
    copy.wait_recv()
    c_all[link.w, link.n] = own + c_recv[...]
    block = c_all.at[link.w, link.n]
    copies = [link.put(block, block, w, link.n) for _, w in link.along_wide()]
    passed = [link.put(block, block, link.w, partner)]
    for (step, _), copy in zip(link.along_wide(), copies):
        copy.wait_recv()
        source = lax.rem(link.w + wide - step, wide)
        block = c_all.at[source, link.n]
        passed.append(link.put(block, block, link.w, partner))
    for copy in passed:
        copy.wait_recv()
    for w in range(wide):
        for n in range(narrow):
            core_ref[w, n * half : (n + 1) * half] = c_all[w, n]
    link.close()


def mode_two_kernel(wide, narrow, p_ref, basis_ref, p_recv, p_all, send, recv):
    link = Link(wide, narrow, send, recv)
    group = wide * narrow
    link.greet()
    copies = [
        link.put(p_ref.at[w * narrow + n], p_recv.at[step], w, n)
        for step, (w, n) in enumerate(link.others())
    ]
    mine = link.w * narrow + link.n
    added = p_ref[mine]
    for step, copy in enumerate(copies):
        copy.wait_recv()
        added = added + p_recv[step]
    p_all[mine] = added
    copies = [link.put(p_all.at[mine], p_all.at[mine], w, n) for w, n in link.others()]
    for copy in copies:
        copy.wait_recv()
    whole = p_all[...].reshape(basis_ref.shape)
    basis_ref[...] = dot_rt(whole, inverse_lower(dot_t(whole, whole)))
    link.close()


def mode_three_kernel(wide, narrow, u_ref, basis_ref, core_ref, u_all, p_send, p_recv, p_all, send, recv):
    link = Link(wide, narrow, send, recv)
    group = wide * narrow
    rows, rank = basis_ref.shape
    share = core_ref.shape[0]
    link.greet()
    copies = [
        link.put(u_ref.at[w * narrow + n], u_all.at[link.n, link.w], w, n) for w, n in link.others()
    ]
    u_all[link.n, link.w] = u_ref[link.w * narrow + link.n]
    for copy in copies:
        copy.wait_recv()
    factor = u_all[0, :, :, share:].reshape(wide * rows, rank)
    unfold = u_all[0, :, :, :share]
    for n in range(1, narrow):
        unfold = unfold + u_all[n, :, :, :share]
    unfold = unfold.reshape(wide * rows, share)
    product = dot(unfold, dot_t(unfold, factor))
    p_send[...] = product.reshape(wide, rows, rank)
    copies = [link.put(p_send.at[w], p_recv.at[step - 1], w, link.n) for step, w in link.along_wide()]
    added = p_send[link.w]
    for step, copy in enumerate(copies):
        copy.wait_recv()
        added = added + p_recv[step]
    p_all[link.n, link.w] = added
    block = p_all.at[link.n, link.w]
    copies = [link.put(block, block, w, n) for w, n in link.others()]
    for copy in copies:
        copy.wait_recv()
    whole = p_all[0]
    for n in range(1, narrow):
        whole = whole + p_all[n]
    p_recv[...] = whole
    whole = whole.reshape(wide * rows, rank)
    inverse = inverse_lower(dot_t(whole, whole))
    basis_ref[...] = dot_rt(p_recv[link.w], inverse)
    core_ref[...] = dot_t(unfold, dot_rt(whole, inverse))
    link.close()


def call(kernel, wide, narrow, outs, scratch, copies, at, operands):
    return pl.pallas_call(
        functools.partial(kernel, wide, narrow),
        out_shape=[jax.ShapeDtypeStruct(shape, jnp.float32) for shape in outs],
        in_specs=[vmem] * len(operands),
        out_specs=[vmem] * len(outs),
        scratch_shapes=[pltpu.VMEM(shape, jnp.float32) for shape in scratch]
        + [pltpu.SemaphoreType.DMA((copies,))] * 2,
        compiler_params=pltpu.CompilerParams(
            collective_id=at, has_side_effects=True, vmem_limit_bytes=32 * 1024 * 1024
        ),
    )(*operands)


def on_device(wide, narrow, window_data, factor_one, factor_two, factor_three):
    layers, rows, cells = window_data.shape
    rank = factor_one.shape[1]
    group = wide * narrow
    per = rank // wide
    share = per * rows
    along_two = contract_high("kij,jb->kbi", window_data, factor_two).reshape(layers, rank * rows)
    unfold_one = contract_high("kc,kn->cn", factor_three, along_two)
    basis_one, core_two = call(
        mode_one_kernel, wide, narrow,
        [(rows, rank), (wide, rank, per * rank)],
        [
            (wide - 1, rank, share), (rank, share),
            (per, rank, rank), (per, rank, rank),
            (wide, rows // wide, rank), (wide - 1, rows // wide, rank), (group, rows // wide, rank),
            (rank, per * rank), (rank // narrow, per * rank), (wide, narrow, rank // narrow, per * rank),
        ],
        4 * (wide - 1) + 3 + group - 1, 0, (unfold_one, factor_one),
    )
    along_one = contract_high("kij,ia->kaj", window_data, basis_one)
    spread_two = contract_high("wcn,kc->kwn", core_two, factor_three).reshape(layers, rank, rank)
    product_two = contract_high("kaj,kba->jb", along_one, spread_two)
    basis_two, = call(
        mode_two_kernel, wide, narrow,
        [(cells, rank)],
        [(group - 1, cells // group, rank), (group, cells // group, rank)],
        2 * (group - 1), 1, (product_two.reshape(group, cells // group, rank),),
    )
    along_new = contract_high("kij,jb->kib", window_data, basis_two)
    unfold_three = contract_high("kib,ia->kba", along_new, basis_one)
    shares = rank // group * rank
    unfold_three = unfold_three.reshape(layers, group, shares)
    unfold_three = jnp.concatenate(
        [unfold_three, jnp.broadcast_to(factor_three[:, None], (layers, group, rank))], axis=2
    ).transpose(1, 0, 2)
    basis_three, core = call(
        mode_three_kernel, wide, narrow,
        [(layers, rank), (shares, rank)],
        [
            (narrow, wide, layers, shares + rank),
            (wide, layers, rank), (wide, layers, rank), (narrow, wide, layers, rank),
        ],
        2 * (group - 1) + wide - 1, 2, (unfold_three,),
    )
    core = core.reshape(rank // group, rank, rank).transpose(1, 0, 2).reshape(rank, shares)
    return basis_one, basis_two, basis_three, core


def orthonormal(basis, gram):
    lower = jnp.linalg.cholesky(gram)
    return lax.linalg.triangular_solve(lower, basis, left_side=False, lower=True, transpose_a=True)


def full_core(partial_value):
    flat = partial_value.reshape(
        partial_value.shape[0], partial_value.shape[1] * partial_value.shape[2]
    )
    shares = lax.psum_scatter(flat, ("wide", "narrow"), scatter_dimension=1, tiled=True)
    whole = lax.all_gather(shares, ("wide", "narrow"), axis=1, tiled=True)
    return whole.reshape(partial_value.shape)


def plain_on_device(window_data, factor_one, factor_two, factor_three):
    rank = factor_one.shape[1]
    along_two = contract("kij,jb->kib", window_data, factor_two)
    unfold_part = contract("kib,kc->ibc", along_two, factor_three).reshape(
        along_two.shape[1], rank * rank
    )
    unfold_rows = lax.psum_scatter(unfold_part, "wide", scatter_dimension=1, tiled=True)
    weights_one = lax.psum(jnp.dot(unfold_rows.T, factor_one, precision=highest), "narrow")
    product_one = lax.psum(jnp.dot(unfold_rows, weights_one, precision=highest), "wide")
    gram_one = lax.psum(jnp.dot(product_one.T, product_one, precision=highest), "narrow")
    basis_one = orthonormal(product_one, gram_one)
    along_one = contract("kij,ia->kaj", window_data, basis_one)
    core_two = full_core(
        contract("kab,kc->abc", contract("kaj,jb->kab", along_one, factor_two), factor_three)
    )
    spread_two = contract("abc,kc->kab", core_two, factor_three)
    product_two = lax.psum(contract("kaj,kab->jb", along_one, spread_two), ("wide", "narrow"))
    basis_two = orthonormal(product_two, jnp.dot(product_two.T, product_two, precision=highest))
    along_new = contract("kij,jb->kib", window_data, basis_two)
    unfold_three = contract("kib,ia->kab", along_new, basis_one)
    core_three = full_core(contract("kab,kc->abc", unfold_three, factor_three))
    product_three = lax.psum(contract("kab,abc->kc", unfold_three, core_three), "narrow")
    gram_three = lax.psum(jnp.dot(product_three.T, product_three, precision=highest), "wide")
    basis_three = orthonormal(product_three, gram_three)
    core_part = contract("kab,kc->abc", unfold_three, basis_three).reshape(rank, rank * rank)
    core_shares = lax.psum_scatter(core_part, ("wide", "narrow"), scatter_dimension=1, tiled=True)
    return (basis_one, basis_two, basis_three, core_shares)


def program(wide, narrow, window_data, factor_one, factor_two, factor_three):
    layers, rows, cells = window_data.shape
    rank = factor_one.shape[1]
    group = wide * narrow
    even = (
        narrow == 2
        and rank % (8 * narrow) == 0
        and rank % group == 0
        and (rank // wide * rows) % 128 == 0
        and rows % (8 * wide) == 0
        and cells % (8 * group) == 0
        and layers % 8 == 0
    )
    body = functools.partial(on_device, wide, narrow) if even else plain_on_device
    return body(window_data, factor_one, factor_two, factor_three)


def solution(mesh):
    return jax.shard_map(
        functools.partial(program, mesh.shape["wide"], mesh.shape["narrow"]),
        mesh=mesh,
        in_specs=(
            P(("win", "wide"), "narrow", None),
            P(("win", "narrow"), None),
            P("win", None),
            P(("win", "wide"), None),
        ),
        out_specs=(
            P(("win", "narrow"), None),
            P("win", None),
            P(("win", "wide"), None),
            P(None, ("win", "wide", "narrow")),
        ),
        check_vma=False,
    )
```

```python
import functools

import jax
import jax.numpy as jnp
from jax import lax
from jax.experimental import pallas as pl
from jax.experimental.pallas import tpu as pltpu
from jax.sharding import PartitionSpec as P

highest = lax.Precision.HIGHEST
vmem = pl.BlockSpec(memory_space=pltpu.VMEM)


def contract(form, left, right):
    return jnp.einsum(form, left, right, precision=highest)


def contract_high(form, left, right):
    return jnp.einsum(form, left, right, precision=lax.Precision.HIGH)


def dot(left, right):
    return jnp.dot(left, right, precision=highest, preferred_element_type=jnp.float32)


def dot_t(left, right):
    return lax.dot_general(
        left, right, (((0,), (0,)), ((), ())), precision=highest, preferred_element_type=jnp.float32
    )


def dot_rt(left, right):
    return lax.dot_general(
        left, right, (((1,), (1,)), ((), ())), precision=highest, preferred_element_type=jnp.float32
    )


def inverse_lower(gram):
    rank = gram.shape[0]
    group = 8
    rows = lax.broadcasted_iota(jnp.int32, (rank, rank), 0)
    columns = lax.broadcasted_iota(jnp.int32, (rank, rank), 1)
    both = jnp.concatenate([gram, (rows == columns).astype(jnp.float32)], axis=1)
    blocks = [both[at : at + group] for at in range(0, rank, group)]
    inside = lax.broadcasted_iota(jnp.int32, (group, 2 * rank), 0)
    wide_shape = (group, 2 * rank)
    for at in range(rank // group):
        later = range(at, rank // group)
        spread = [
            {k: jnp.broadcast_to(blocks[k][:, at * group + t : at * group + t + 1], wide_shape) for k in later}
            for t in range(group)
        ]
        pivots = jnp.ones(wide_shape, jnp.float32)
        for row in range(group):
            pivot = spread[row][at][row : row + 1]
            pivots = jnp.where(inside == row, pivot, pivots)
            over = 1.0 / pivot
            column = dict(spread[row])
            column[at] = jnp.where(inside > row, column[at], 0.0)
            for t in range(row + 1, group):
                factor = spread[t][at][row : row + 1] * over
                spread[t] = {k: spread[t][k] - column[k] * factor for k in later}
            scaled = blocks[at][row : row + 1] * over
            for k in later:
                blocks[k] = blocks[k] - column[k] * scaled
        blocks[at] = blocks[at] * lax.rsqrt(pivots)
    return jnp.concatenate(blocks, axis=0)[:, rank:]


class Link:
    def __init__(self, wide, narrow, send, recv):
        self.wide, self.narrow = wide, narrow
        self.send, self.recv = send, recv
        self.used = 0
        self.started = []
        self.w = lax.axis_index("wide")
        self.n = lax.axis_index("narrow")

    def others(self):
        for step in range(1, self.wide * self.narrow):
            dw, dn = divmod(step, self.narrow)
            yield lax.rem(self.w + dw, self.wide), lax.rem(self.n + dn, self.narrow)

    def greet(self):
        barrier = pltpu.get_barrier_semaphore()
        for w, n in self.others():
            pl.semaphore_signal(
                barrier, inc=1, device_id={"wide": w, "narrow": n}, device_id_type=pl.DeviceIdType.MESH
            )
        pl.semaphore_wait(barrier, self.wide * self.narrow - 1)

    def put(self, source, target, w, n):
        copy = pltpu.make_async_remote_copy(
            src_ref=source,
            dst_ref=target,
            send_sem=self.send.at[self.used],
            recv_sem=self.recv.at[self.used],
            device_id={"wide": w, "narrow": n},
            device_id_type=pl.DeviceIdType.MESH,
        )
        self.used += 1
        copy.start()
        self.started.append(copy)
        return copy

    def along_wide(self):
        return [(step, lax.rem(self.w + step, self.wide)) for step in range(1, self.wide)]

    def close(self):
        for copy in self.started:
            copy.wait_send()


def mode_one_kernel(wide, narrow, u_ref, f_ref, basis_ref, core_ref,
                    parts, total, w_send, w_recv, p_send, p_recv, p_all, c_part, c_recv, c_all, send, recv):
    link = Link(wide, narrow, send, recv)
    share = total.shape[1]
    rows = f_ref.shape[0]
    rank = f_ref.shape[1]
    per = rank // wide
    chunk = rows // wide
    half = rank // narrow
    link.greet()
    partner = lax.rem(link.n + 1, narrow)
    copies = []
    for step, w in link.along_wide():
        columns = pl.ds(pl.multiple_of(w * share, 128), share)
        copies.append(link.put(u_ref.at[:, columns], parts.at[step - 1], w, link.n))
    added = u_ref[:, pl.ds(pl.multiple_of(link.w * share, 128), share)]
    for step, copy in enumerate(copies):
        copy.wait_recv()
        added = added + parts[step]
    total[...] = added
    factor = f_ref[...]
    for v in range(per):
        w_send[v] = dot(total[:, v * rows : (v + 1) * rows], factor)
    copy = link.put(w_send, w_recv, link.w, partner)
    copy.wait_recv()
    product = jnp.zeros((rows, rank), jnp.float32)
    for v in range(per):
        product = product + dot_t(total[:, v * rows : (v + 1) * rows], w_send[v] + w_recv[v])
    for w in range(wide):
        p_send[w] = product[w * chunk : (w + 1) * chunk]
    copies = [link.put(p_send.at[w], p_recv.at[step - 1], w, link.n) for step, w in link.along_wide()]
    added = p_send[link.w]
    for step, copy in enumerate(copies):
        copy.wait_recv()
        added = added + p_recv[step]
    mine = link.n * wide + link.w
    p_all[mine] = added
    copies = [link.put(p_all.at[mine], p_all.at[mine], w, n) for w, n in link.others()]
    for copy in copies:
        copy.wait_recv()
    whole = p_all[...].reshape(narrow * rows, rank)
    inverse = inverse_lower(dot_t(whole, whole))
    basis = dot_rt(p_all[pl.ds(link.n * wide, wide)].reshape(rows, rank), inverse)
    basis_ref[...] = basis
    for v in range(per):
        c_part[:, v * rank : (v + 1) * rank] = dot(total[:, v * rows : (v + 1) * rows], basis)
    theirs = pl.ds(pl.multiple_of(partner * half, 8), half)
    copy = link.put(c_part.at[theirs, :], c_recv, link.w, partner)
    own = c_part[pl.ds(pl.multiple_of(link.n * half, 8), half), :]
    copy.wait_recv()
    c_all[link.w, link.n] = own + c_recv[...]
    block = c_all.at[link.w, link.n]
    copies = [link.put(block, block, w, link.n) for _, w in link.along_wide()]
    passed = [link.put(block, block, link.w, partner)]
    for (step, _), copy in zip(link.along_wide(), copies):
        copy.wait_recv()
        source = lax.rem(link.w + wide - step, wide)
        block = c_all.at[source, link.n]
        passed.append(link.put(block, block, link.w, partner))
    for copy in passed:
        copy.wait_recv()
    for w in range(wide):
        for n in range(narrow):
            core_ref[w, n * half : (n + 1) * half] = c_all[w, n]
    link.close()


def mode_two_kernel(wide, narrow, p_ref, basis_ref, p_recv, p_all, send, recv):
    link = Link(wide, narrow, send, recv)
    group = wide * narrow
    link.greet()
    copies = [
        link.put(p_ref.at[w * narrow + n], p_recv.at[step], w, n)
        for step, (w, n) in enumerate(link.others())
    ]
    mine = link.w * narrow + link.n
    added = p_ref[mine]
    for step, copy in enumerate(copies):
        copy.wait_recv()
        added = added + p_recv[step]
    p_all[mine] = added
    copies = [link.put(p_all.at[mine], p_all.at[mine], w, n) for w, n in link.others()]
    for copy in copies:
        copy.wait_recv()
    whole = p_all[...].reshape(basis_ref.shape)
    basis_ref[...] = dot_rt(whole, inverse_lower(dot_t(whole, whole)))
    link.close()


def mode_three_kernel(wide, narrow, u_ref, basis_ref, core_ref, u_all, p_send, p_recv, p_all, send, recv):
    link = Link(wide, narrow, send, recv)
    group = wide * narrow
    rows, rank = basis_ref.shape
    share = core_ref.shape[0]
    link.greet()
    copies = [
        link.put(u_ref.at[w * narrow + n], u_all.at[link.n, link.w], w, n) for w, n in link.others()
    ]
    u_all[link.n, link.w] = u_ref[link.w * narrow + link.n]
    for copy in copies:
        copy.wait_recv()
    factor = u_all[0, :, :, share:].reshape(wide * rows, rank)
    unfold = u_all[0, :, :, :share]
    for n in range(1, narrow):
        unfold = unfold + u_all[n, :, :, :share]
    unfold = unfold.reshape(wide * rows, share)
    product = dot(unfold, dot_t(unfold, factor))
    p_send[...] = product.reshape(wide, rows, rank)
    copies = [link.put(p_send.at[w], p_recv.at[step - 1], w, link.n) for step, w in link.along_wide()]
    added = p_send[link.w]
    for step, copy in enumerate(copies):
        copy.wait_recv()
        added = added + p_recv[step]
    p_all[link.n, link.w] = added
    block = p_all.at[link.n, link.w]
    copies = [link.put(block, block, w, n) for w, n in link.others()]
    for copy in copies:
        copy.wait_recv()
    whole = p_all[0]
    for n in range(1, narrow):
        whole = whole + p_all[n]
    p_recv[...] = whole
    whole = whole.reshape(wide * rows, rank)
    inverse = inverse_lower(dot_t(whole, whole))
    basis_ref[...] = dot_rt(p_recv[link.w], inverse)
    core_ref[...] = dot_t(unfold, dot_rt(whole, inverse))
    link.close()


def call(kernel, wide, narrow, outs, scratch, copies, at, operands):
    return pl.pallas_call(
        functools.partial(kernel, wide, narrow),
        out_shape=[jax.ShapeDtypeStruct(shape, jnp.float32) for shape in outs],
        in_specs=[vmem] * len(operands),
        out_specs=[vmem] * len(outs),
        scratch_shapes=[pltpu.VMEM(shape, jnp.float32) for shape in scratch]
        + [pltpu.SemaphoreType.DMA((copies,))] * 2,
        compiler_params=pltpu.CompilerParams(
            collective_id=at, has_side_effects=True, vmem_limit_bytes=32 * 1024 * 1024
        ),
    )(*operands)


def on_device(wide, narrow, window_data, factor_one, factor_two, factor_three):
    layers, rows, cells = window_data.shape
    rank = factor_one.shape[1]
    group = wide * narrow
    per = rank // wide
    share = per * rows
    along_two = contract_high("kij,jb->kbi", window_data, factor_two).reshape(layers, rank * rows)
    unfold_one = contract_high("kc,kn->cn", factor_three, along_two)
    basis_one, core_two = call(
        mode_one_kernel, wide, narrow,
        [(rows, rank), (wide, rank, per * rank)],
        [
            (wide - 1, rank, share), (rank, share),
            (per, rank, rank), (per, rank, rank),
            (wide, rows // wide, rank), (wide - 1, rows // wide, rank), (group, rows // wide, rank),
            (rank, per * rank), (rank // narrow, per * rank), (wide, narrow, rank // narrow, per * rank),
        ],
        4 * (wide - 1) + 3 + group - 1, 0, (unfold_one, factor_one),
    )
    spread_two = contract_high("wcn,kc->kwn", core_two, factor_three).reshape(layers, rank, rank)
    spread_two = contract_high("kba,ia->kib", spread_two, basis_one)
    product_two = contract_high("kij,kib->jb", window_data, spread_two)
    basis_two, = call(
        mode_two_kernel, wide, narrow,
        [(cells, rank)],
        [(group - 1, cells // group, rank), (group, cells // group, rank)],
        2 * (group - 1), 1, (product_two.reshape(group, cells // group, rank),),
    )
    along_new = contract_high("kij,jb->kib", window_data, basis_two)
    unfold_three = contract_high("kib,ia->kba", along_new, basis_one)
    shares = rank // group * rank
    unfold_three = unfold_three.reshape(layers, group, shares)
    unfold_three = jnp.concatenate(
        [unfold_three, jnp.broadcast_to(factor_three[:, None], (layers, group, rank))], axis=2
    ).transpose(1, 0, 2)
    basis_three, core = call(
        mode_three_kernel, wide, narrow,
        [(layers, rank), (shares, rank)],
        [
            (narrow, wide, layers, shares + rank),
            (wide, layers, rank), (wide, layers, rank), (narrow, wide, layers, rank),
        ],
        2 * (group - 1) + wide - 1, 2, (unfold_three,),
    )
    core = core.reshape(rank // group, rank, rank).transpose(1, 0, 2).reshape(rank, shares)
    return basis_one, basis_two, basis_three, core


def orthonormal(basis, gram):
    lower = jnp.linalg.cholesky(gram)
    return lax.linalg.triangular_solve(lower, basis, left_side=False, lower=True, transpose_a=True)


def full_core(partial_value):
    flat = partial_value.reshape(
        partial_value.shape[0], partial_value.shape[1] * partial_value.shape[2]
    )
    shares = lax.psum_scatter(flat, ("wide", "narrow"), scatter_dimension=1, tiled=True)
    whole = lax.all_gather(shares, ("wide", "narrow"), axis=1, tiled=True)
    return whole.reshape(partial_value.shape)


def plain_on_device(window_data, factor_one, factor_two, factor_three):
    rank = factor_one.shape[1]
    along_two = contract("kij,jb->kib", window_data, factor_two)
    unfold_part = contract("kib,kc->ibc", along_two, factor_three).reshape(
        along_two.shape[1], rank * rank
    )
    unfold_rows = lax.psum_scatter(unfold_part, "wide", scatter_dimension=1, tiled=True)
    weights_one = lax.psum(jnp.dot(unfold_rows.T, factor_one, precision=highest), "narrow")
    product_one = lax.psum(jnp.dot(unfold_rows, weights_one, precision=highest), "wide")
    gram_one = lax.psum(jnp.dot(product_one.T, product_one, precision=highest), "narrow")
    basis_one = orthonormal(product_one, gram_one)
    along_one = contract("kij,ia->kaj", window_data, basis_one)
    core_two = full_core(
        contract("kab,kc->abc", contract("kaj,jb->kab", along_one, factor_two), factor_three)
    )
    spread_two = contract("abc,kc->kab", core_two, factor_three)
    product_two = lax.psum(contract("kaj,kab->jb", along_one, spread_two), ("wide", "narrow"))
    basis_two = orthonormal(product_two, jnp.dot(product_two.T, product_two, precision=highest))
    along_new = contract("kij,jb->kib", window_data, basis_two)
    unfold_three = contract("kib,ia->kab", along_new, basis_one)
    core_three = full_core(contract("kab,kc->abc", unfold_three, factor_three))
    product_three = lax.psum(contract("kab,abc->kc", unfold_three, core_three), "narrow")
    gram_three = lax.psum(jnp.dot(product_three.T, product_three, precision=highest), "wide")
    basis_three = orthonormal(product_three, gram_three)
    core_part = contract("kab,kc->abc", unfold_three, basis_three).reshape(rank, rank * rank)
    core_shares = lax.psum_scatter(core_part, ("wide", "narrow"), scatter_dimension=1, tiled=True)
    return (basis_one, basis_two, basis_three, core_shares)


def program(wide, narrow, window_data, factor_one, factor_two, factor_three):
    layers, rows, cells = window_data.shape
    rank = factor_one.shape[1]
    group = wide * narrow
    even = (
        narrow == 2
        and rank % (8 * narrow) == 0
        and rank % group == 0
        and (rank // wide * rows) % 128 == 0
        and rows % (8 * wide) == 0
        and cells % (8 * group) == 0
        and layers % 8 == 0
    )
    body = functools.partial(on_device, wide, narrow) if even else plain_on_device
    return body(window_data, factor_one, factor_two, factor_three)


def solution(mesh):
    return jax.shard_map(
        functools.partial(program, mesh.shape["wide"], mesh.shape["narrow"]),
        mesh=mesh,
        in_specs=(
            P(("win", "wide"), "narrow", None),
            P(("win", "narrow"), None),
            P("win", None),
            P(("win", "wide"), None),
        ),
        out_specs=(
            P(("win", "narrow"), None),
            P("win", None),
            P(("win", "wide"), None),
            P(None, ("win", "wide", "narrow")),
        ),
        check_vma=False,
    )
```
